32 devices in a mesh: seq: 4 (over y, core), fsdp: 4 (over z), replica: 2 (over x).
Axes of the slice: x: 2, y: 2, z: 4, core: 2. Of those that a mesh axis runs over, the one named last changes fastest.
Arguments:
- inputs: bfloat16 [32, 1024, 768], P(('fsdp', 'replica'), 'seq'), may hold values from -6 to 6
- segments: int32 [32, 1024], P(('fsdp', 'replica')), may hold values from 0 to 15, as said below
- cotangent: bfloat16 [32, 1024, 768], P(('fsdp', 'replica'), 'seq'), may hold values from -6 to 6
- w_rows: float32 [768, 6144], P('fsdp')
- m_rows: float32 [768, 6144], P('fsdp')
- v_rows: float32 [768, 6144], P('fsdp')
- w_down: float32 [3072, 768], P('fsdp'), may hold values from -0.109375 to 0.109375
- m_down: float32 [3072, 768], P('fsdp')
- v_down: float32 [3072, 768], P('fsdp')
- smalls: float32 [12, 768], P(None, 'fsdp')
- m_small: float32 [12, 768], P(None, 'fsdp')
- v_small: float32 [12, 768], P(None, 'fsdp')
Outputs:
- activations: bfloat16 [32, 1024, 768], P(('fsdp', 'replica'), 'seq')
- input_grad: float32 [32, 1024, 768], P(('fsdp', 'replica'), 'seq')
- new_rows: float32 [768, 6144], P('fsdp')
- moment_rows: float32 [768, 6144], P('fsdp')
- second_rows: float32 [768, 6144], P('fsdp')
- new_down: float32 [3072, 768], P('fsdp')
- moment_down: float32 [3072, 768], P('fsdp')
- second_down: float32 [3072, 768], P('fsdp')
- new_small: float32 [12, 768], P(None, 'fsdp')
- moment_small: float32 [12, 768], P(None, 'fsdp')
- second_small: float32 [12, 768], P(None, 'fsdp')
The draws below stay inside these ranges and needn't reach their ends.
Inputs may be any that keep to these rules, and one draw needn't show every extreme that they name: `segments`: in each sequence the document numbers start at 0, never fall and rise by at most one from a position to the next; every document but a sequence's last holds 64 to 800 positions; of the 4 sequences of one index pair of fsdp and replica, one is a single document; one sequence in all consists of 16 documents of 64 positions each.
All inputs are finite; a program needn't handle non-finite values.
Results may differ from the reference program's by a relative error of at most 0.023.
Values may be sent and summed in bfloat16 or wider, within the bound.
A program may use at most 320 MiB of HBM per device.

```python
import math
import jax
import jax.numpy as jnp
from jax import lax

D = 768
H = 12
FF = 3072
LEN = 1024
SEQ_DEV = 4
STEP = 10
SEQS = 32


def token_root():
    return math.sqrt(SEQS * LEN)


def row_scales():
    parts_list = [jnp.full((3 * D,), 1.0, jnp.float32), jnp.full((D,), 0.2, jnp.float32), jnp.full((FF,), 0.5, jnp.float32)]
    return jnp.concatenate(parts_list) * token_root()


def first_moment(key, array_shape, grad_size):
    return jax.random.normal(key, array_shape, jnp.float32) * grad_size * (0.1 / 0.9)


def second_moment(key, array_shape, grad_size):
    factor = jnp.exp(jax.random.uniform(key, array_shape, jnp.float32, 0.0, math.log(4.0)))
    return factor * grad_size * grad_size * (0.001 / 0.999)


def draw_segments(key, part):
    key = jax.random.fold_in(key, 11)
    key_lengths, key_choice = jax.random.split(key)
    doc_lengths = jax.random.randint(key_lengths, (SEQS, 17), LEN // 16, LEN * 25 // 32 + 1)
    doc_ends = jnp.cumsum(doc_lengths, axis=1)
    places = jnp.arange(LEN, dtype=jnp.int32)
    doc_ids = jnp.sum((doc_ends[:, None, :] <= places[None, :, None]).astype(jnp.int32), axis=2)
    chosen = jax.random.randint(key_choice, (SEQS // SEQ_DEV,), 0, SEQ_DEV)
    seq_index = jnp.arange(SEQS, dtype=jnp.int32)
    single = seq_index % SEQ_DEV == jnp.repeat(chosen, SEQ_DEV)
    many_index = (chosen[0] + 1) % SEQ_DEV
    many = seq_index == many_index
    even_ids = (places // (LEN // 16)).astype(jnp.int32)
    doc_ids = jnp.where(many[:, None], even_ids[None, :], doc_ids)
    return jnp.where(single[:, None], 0, doc_ids).astype(jnp.int32)


def draw_w_rows(key, part):
    key = jax.random.fold_in(key, 2)
    columns = jnp.arange(4 * D + FF)
    column_std = jnp.where((columns >= 3 * D) & (columns < 4 * D), 4.0 * D ** (-0.5), D ** (-0.5))
    return jax.random.normal(key, (D, 4 * D + FF), jnp.float32) * column_std


def draw_m_rows(key, part):
    key = jax.random.fold_in(key, 3)
    return first_moment(key, (D, 4 * D + FF), row_scales())


def draw_v_rows(key, part):
    key = jax.random.fold_in(key, 4)
    return second_moment(key, (D, 4 * D + FF), row_scales())


def draw_m_down(key, part):
    key = jax.random.fold_in(key, 5)
    return first_moment(key, (FF, D), 0.5 * token_root())


def draw_v_down(key, part):
    key = jax.random.fold_in(key, 6)
    return second_moment(key, (FF, D), 0.5 * token_root())


def draw_smalls(key, part):
    key = jax.random.fold_in(key, 7)
    key_bias, key_gain = jax.random.split(key)
    biases = jax.random.normal(key_bias, (8 + FF // D, D), jnp.float32) * 0.3
    gains = jax.random.uniform(key_gain, (8 + FF // D, D), jnp.float32, 0.5, 1.5)
    row_index = jnp.arange(8 + FF // D)
    is_gain = (row_index == 0) | (row_index == 5)
    return jnp.where(is_gain[:, None], gains, biases)


def draw_m_small(key, part):
    key = jax.random.fold_in(key, 8)
    return first_moment(key, (8 + FF // D, D), token_root())


def draw_v_small(key, part):
    key = jax.random.fold_in(key, 9)
    return second_moment(key, (8 + FF // D, D), token_root())


def steps_of(rng, dims, cuts, least, top_value):
    factor_of = 1.0
    for position, blocks in cuts:
        draws = jax.random.uniform(jax.random.fold_in(jax.random.fold_in(rng, 6), position), (blocks,), jnp.float32, least / len(cuts), top_value / len(cuts))
        factor_of = factor_of * jnp.repeat(jnp.exp(draws), dims[position] // blocks).reshape((-1,) + (1,) * (len(dims) - 1 - position))
    return factor_of


def scatter_about(rng, dims, scale, limit, cuts=(), kind=jnp.bfloat16):
    array = jax.random.normal(rng, dims, jnp.float32) * scale
    if len(cuts) > 0:
        array = steps_of(rng, dims, cuts, -0.22, 0.18) * array
    return jnp.clip(array, min=-limit, max=limit).astype(kind)


def setup_inputs(seed: int = 0) -> dict:
    streams_of = jax.random.split(jax.random.key(seed), 13)
    return {
        "inputs": scatter_about(streams_of[0], (SEQS, LEN, D), 1.0, 6.0, ((0, 8), (1, 4))),
        "segments": draw_segments(jax.random.fold_in(streams_of[12], 71), 0),
        "cotangent": scatter_about(streams_of[2], (SEQS, LEN, D), 1.0, 6.0, ((0, 8), (1, 4))),
        "w_rows": draw_w_rows(jax.random.fold_in(streams_of[12], 71), 0),
        "m_rows": draw_m_rows(jax.random.fold_in(streams_of[12], 71), 0),
        "v_rows": draw_v_rows(jax.random.fold_in(streams_of[12], 71), 0),
        "w_down": scatter_about(streams_of[6], (FF, D), FF ** -0.5, 0.109375, ((0, 4),), jnp.float32),
        "m_down": draw_m_down(jax.random.fold_in(streams_of[12], 71), 0),
        "v_down": draw_v_down(jax.random.fold_in(streams_of[12], 71), 0),
        "smalls": draw_smalls(jax.random.fold_in(streams_of[12], 71), 0),
        "m_small": draw_m_small(jax.random.fold_in(streams_of[12], 71), 0),
        "v_small": draw_v_small(jax.random.fold_in(streams_of[12], 71), 0),
    }


@jax.custom_vjp
def low(v):
    return lax.optimization_barrier(v.astype(jnp.bfloat16)).astype(jnp.float32)

@jax.custom_vjp
def low_back(v):
    return v

def low_keep(v):
    return (low(v), None)

def low_pass(kept, grad):
    return (grad,)

def back_keep(v):
    return (v, None)

def back_low(kept, grad):
    return (low(grad),)
low.defvjp(low_keep, low_pass)
low_back.defvjp(back_keep, back_low)
epsilon = 1e-05
beta_first = 0.9
beta_second = 0.999
adam_epsilon = 1e-08
weight_decay = 0.1
rate_rows = 0.08
rate_down = 0.04
rate_small = 0.5
masked_score = -1e+30
highest = lax.Precision.HIGHEST

def normalize(values, norm_gain, norm_shift):
    centered = values - lax.optimization_barrier(jnp.mean(values, axis=-1, keepdims=True))
    spread = lax.optimization_barrier(jnp.mean(centered * centered, axis=-1, keepdims=True))
    return centered * lax.rsqrt(spread + epsilon) * norm_gain + norm_shift

def adam_update(weight, moment, second, gradient, step_rate, decay_rate):
    moment_new = beta_first * moment + (1.0 - beta_first) * gradient
    second_new = beta_second * second + (1.0 - beta_second) * gradient * gradient
    moment_hat = moment_new / (1.0 - beta_first ** STEP)
    second_hat = second_new / (1.0 - beta_second ** STEP)
    weight_new = weight - step_rate * (moment_hat / (jnp.sqrt(second_hat) + adam_epsilon) + decay_rate * weight)
    return (weight_new, moment_new, second_new)

def forward(features, doc_ids, w_rows, w_down, smalls):
    w_rows = low(w_rows)
    w_down = low(w_down)
    smalls = low(smalls)
    seq_count, seq_length, model_width = features.shape
    head_size = model_width // H
    bias_up = smalls[8:].reshape(-1)
    normed = low(normalize(features, smalls[0], smalls[1]))
    projected = jnp.einsum('bld,de->ble', normed, w_rows[:, :3 * model_width], precision=highest)
    queries = low(low_back(projected[..., :model_width]) + smalls[2])
    keys_all = low(low_back(projected[..., model_width:2 * model_width]))
    values_all = low(low_back(projected[..., 2 * model_width:]) + smalls[3])
    query_heads = queries.reshape(seq_count, seq_length, H, head_size)
    key_heads = keys_all.reshape(seq_count, seq_length, H, head_size)
    value_heads = values_all.reshape(seq_count, seq_length, H, head_size)
    scores = low_back(jnp.einsum('bqhe,bkhe->bhqk', query_heads, key_heads, precision=highest) * head_size ** (-0.5))
    places = jnp.arange(seq_length, dtype=jnp.int32)
    allowed = (places[:, None] >= places[None, :])[None] & (doc_ids[:, :, None] == doc_ids[:, None, :])
    scores = jnp.where(allowed[:, None], scores, masked_score)
    largest = lax.optimization_barrier(jnp.max(scores, axis=-1, keepdims=True))
    weights = jnp.exp(scores - largest)
    probabilities = low(weights / lax.optimization_barrier(jnp.sum(weights, axis=-1, keepdims=True)))
    attended = jnp.einsum('bhqk,bkhe->bqhe', probabilities, value_heads, precision=highest)
    attended = low(low_back(attended.reshape(seq_count, seq_length, model_width)))
    residual = features + (low_back(jnp.einsum('bld,de->ble', attended, w_rows[:, 3 * model_width:4 * model_width], precision=highest)) + smalls[4])
    normed_two = low(normalize(residual, smalls[5], smalls[6]))
    hidden = low_back(jnp.einsum('bld,df->blf', normed_two, w_rows[:, 4 * model_width:], precision=highest)) + bias_up
    active = low(jax.nn.gelu(hidden, approximate=True))
    output = low_back(jnp.einsum('blf,fd->bld', active, w_down, precision=highest)) + smalls[7]
    return residual + output

def reference(inputs, segments, cotangent, w_rows, m_rows, v_rows, w_down, m_down, v_down, smalls, m_small, v_small):
    group_size = math.gcd(SEQS, max(1, 4096 // LEN))
    block_count = SEQS // group_size
    input_blocks = inputs.astype(jnp.float32).reshape(block_count, group_size, LEN, D)
    segment_blocks = segments.reshape(block_count, group_size, LEN)
    cotangent_blocks = cotangent.astype(jnp.float32).reshape(block_count, group_size, LEN, D)

    def one_block(totals, block_data):
        block_inputs, block_segments, block_cotangent = block_data

        def local_forward(values, row_weights, down_weights, small_weights):
            return forward(values, block_segments, row_weights, down_weights, small_weights)
        result, pullback = jax.vjp(local_forward, block_inputs, w_rows, w_down, smalls)
        grad_inputs, grad_rows, down_weight_gradient, grad_small = pullback(block_cotangent)
        totals = (totals[0] + grad_rows, totals[1] + down_weight_gradient, totals[2] + grad_small)
        return (totals, (result.astype(jnp.bfloat16), grad_inputs))
    initial = (jnp.zeros(w_rows.shape, jnp.float32), jnp.zeros(w_down.shape, jnp.float32), jnp.zeros(smalls.shape, jnp.float32))
    totals, (outputs, input_grads) = lax.scan(one_block, initial, (input_blocks, segment_blocks, cotangent_blocks))
    activations = outputs.reshape(SEQS, LEN, D)
    input_grad = input_grads.reshape(SEQS, LEN, D)
    new_rows, moment_rows, second_rows = adam_update(w_rows, m_rows, v_rows, totals[0], rate_rows, weight_decay)
    new_down, moment_down, second_down = adam_update(w_down, m_down, v_down, totals[1], rate_down, weight_decay)
    new_small, moment_small, second_small = adam_update(smalls, m_small, v_small, totals[2], rate_small, 0.0)
    return (activations, input_grad, new_rows, moment_rows, second_rows, new_down, moment_down, second_down, new_small, moment_small, second_small)
```

```python
import functools

import jax
import jax.numpy as jnp
from jax import lax
from jax.experimental import pallas as pl
from jax.experimental.pallas import tpu as pltpu
from jax.sharding import PartitionSpec as P

H = 12
STEP = 10


epsilon = 1e-05
beta_first = 0.9
beta_second = 0.999
adam_epsilon = 1e-08
weight_decay = 0.1
rate_rows = 0.08
rate_down = 0.04
rate_small = 0.5
masked_score = -1e30


def normalize(values, norm_gain, norm_shift):
    centered = values - jnp.mean(values, axis=-1, keepdims=True)
    spread = jnp.mean(centered * centered, axis=-1, keepdims=True)
    return centered * lax.rsqrt(spread + epsilon) * norm_gain + norm_shift


def smooth_gelu(values):
    return jax.nn.gelu(values, approximate=True)


def adam_update(weight, moment, second, gradient, step_rate, decay_rate):
    moment_new = beta_first * moment + (1.0 - beta_first) * gradient
    second_new = beta_second * second + (1.0 - beta_second) * gradient * gradient
    moment_hat = moment_new / (1.0 - beta_first**STEP)
    second_hat = second_new / (1.0 - beta_second**STEP)
    weight_new = weight - step_rate * (
        moment_hat / (jnp.sqrt(second_hat) + adam_epsilon) + decay_rate * weight
    )
    return (weight_new, moment_new, second_new)


LANES = 128
BLOCK = 256


def lane_masks(head_width):
    lane = lax.broadcasted_iota(jnp.int32, (1, LANES), 1)
    return [
        ((lane >= start) & (lane < start + head_width)).astype(jnp.float32).astype(jnp.bfloat16)
        for start in range(0, LANES, head_width)
    ]


def transposed(values):
    return values.astype(jnp.float32).T.astype(jnp.bfloat16)


def dot_lanes(left, right):
    return lax.dot_general(
        left, right, (((1,), (1,)), ((), ())), preferred_element_type=jnp.float32
    )


def dot_plain(left, right):
    return jnp.dot(left, right, preferred_element_type=jnp.float32)


def mask_bias(places_col, places_row, start, stop):
    key_segments = places_col[:stop]
    query_segments = places_row[:, start:stop]
    key_places = lax.broadcasted_iota(jnp.int32, (stop, stop - start), 0)
    query_places = start + lax.broadcasted_iota(jnp.int32, (stop, stop - start), 1)
    allowed = (key_segments == query_segments) & (key_places <= query_places)
    return jnp.where(allowed, 0.0, masked_score)


def attend_kernel(head_width, q_ref, k_ref, v_ref, row_ref, col_ref, out_ref):
    length = q_ref.shape[1]
    keys = k_ref[0]
    values_t = transposed(v_ref[0])
    masks = lane_masks(head_width)
    scale = head_width ** (-0.5)
    for start in range(0, length, BLOCK):
        stop = start + BLOCK
        bias = mask_bias(col_ref[0], row_ref[0], start, stop)
        queries = q_ref[0, start:stop, :] * jnp.bfloat16(scale)
        parts = []
        for head, mask in enumerate(masks):
            scores = dot_lanes(keys[:stop], queries * mask) + bias
            largest = jnp.max(scores, axis=0, keepdims=True)
            weights = jnp.exp(scores - largest)
            totals = jnp.sum(weights, axis=0, keepdims=True)
            low = head * head_width
            mixed = dot_plain(
                values_t[low : low + head_width, :stop], weights.astype(jnp.bfloat16)
            )
            parts.append(mixed / totals)
        out_ref[0, start:stop, :] = jnp.concatenate(parts, axis=0).T.astype(jnp.bfloat16)


def attend_back_kernel(
    head_width, q_ref, k_ref, v_ref, g_ref, row_ref, col_ref, dq_ref, dk_ref, dv_ref, dk_sum, dv_sum
):
    length = q_ref.shape[1]
    keys = k_ref[0]
    values = v_ref[0]
    keys_t = transposed(keys)
    masks = lane_masks(head_width)
    scale = head_width ** (-0.5)
    dk_sum[...] = jnp.zeros_like(dk_sum)
    dv_sum[...] = jnp.zeros_like(dv_sum)
    for start in range(0, length, BLOCK):
        stop = start + BLOCK
        bias = mask_bias(col_ref[0], row_ref[0], start, stop)
        queries = q_ref[0, start:stop, :] * jnp.bfloat16(scale)
        grads = g_ref[0, start:stop, :]
        dq_parts, probs_parts, ds_parts = [], [], []
        query_heads = [queries * mask for mask in masks]
        grad_heads = [grads * mask for mask in masks]
        for head in range(len(masks)):
            scores = dot_lanes(keys[:stop], query_heads[head]) + bias
            largest = jnp.max(scores, axis=0, keepdims=True)
            weights = jnp.exp(scores - largest)
            totals = jnp.sum(weights, axis=0, keepdims=True)
            probs = weights * (1.0 / totals)
            grad_probs = dot_lanes(values[:stop], grad_heads[head])
            centered = jnp.sum(probs * grad_probs, axis=0, keepdims=True)
            grad_scores = (probs * (grad_probs - centered)).astype(jnp.bfloat16)
            low = head * head_width
            dq_parts.append(dot_plain(keys_t[low : low + head_width, :stop], grad_scores))
            ds_parts.append(grad_scores)
            probs_parts.append(probs.astype(jnp.bfloat16))
        dk_sum[:stop, :] += dot_plain(
            jnp.concatenate(ds_parts, axis=1), jnp.concatenate(query_heads, axis=0)
        )
        dv_sum[:stop, :] += dot_plain(
            jnp.concatenate(probs_parts, axis=1), jnp.concatenate(grad_heads, axis=0)
        )
        dq = jnp.concatenate(dq_parts, axis=0) * scale
        dq_ref[0, start:stop, :] = dq.T.astype(jnp.bfloat16)
    dk_ref[0] = dk_sum[...].astype(jnp.bfloat16)
    dv_ref[0] = dv_sum[...].astype(jnp.bfloat16)


def attention_specs(length, groups):
    def column(offset):
        return pl.BlockSpec((1, length, LANES), lambda n, j: (n, 0, offset * groups + j))

    row = pl.BlockSpec((1, 1, length), lambda n, j: (n, 0, 0))
    col = pl.BlockSpec((1, length, 1), lambda n, j: (n, 0, 0))
    return column, row, col


def attend(mixed, rows, cols):
    count, length, width = mixed.shape
    width //= 3
    groups = width // LANES
    column, row, col = attention_specs(length, groups)
    return pl.pallas_call(
        functools.partial(attend_kernel, width // H),
        grid=(count, groups),
        in_specs=[column(0), column(1), column(2), row, col],
        out_specs=column(0),
        out_shape=jax.ShapeDtypeStruct((count, length, width), jnp.bfloat16),
        compiler_params=pltpu.CompilerParams(vmem_limit_bytes=48 * 2**20),
        cost_estimate=pl.CostEstimate(
            flops=3 * count * length * length * width,
            bytes_accessed=8 * count * length * width,
            transcendentals=count * H * length * length // 2,
        ),
    )(mixed, mixed, mixed, rows, cols)


def attend_back(mixed, grads, rows, cols):
    count, length, width = grads.shape
    groups = width // LANES
    column, row, col = attention_specs(length, groups)
    shape = jax.ShapeDtypeStruct((count, length, width), jnp.bfloat16)
    return pl.pallas_call(
        functools.partial(attend_back_kernel, width // H),
        grid=(count, groups),
        in_specs=[column(0), column(1), column(2), column(0), row, col],
        out_specs=[column(0)] * 3,
        out_shape=[shape] * 3,
        scratch_shapes=[pltpu.VMEM((length, LANES), jnp.float32)] * 2,
        compiler_params=pltpu.CompilerParams(vmem_limit_bytes=48 * 2**20),
        cost_estimate=pl.CostEstimate(
            flops=7 * count * length * length * width,
            bytes_accessed=14 * count * length * width,
            transcendentals=count * H * length * length // 2,
        ),
    )(mixed, mixed, mixed, grads, rows, cols)


def partner(values, axis, bit):
    size = lax.axis_size(axis)
    return lax.ppermute(values, axis, [(i, i ^ bit) for i in range(size)])


def half_of(values, upper, dim):
    half = values.shape[dim] // 2
    return lax.dynamic_slice_in_dim(values, upper * half, half, dim)


def gather_columns(values, extra=None):
    upper = lax.axis_index("seq") & 1
    own = half_of(values, upper, 1)
    width = own.shape[1]
    if extra is not None:
        own = jnp.concatenate([own, extra], axis=1)
    full = lax.all_gather(own, "fsdp", axis=0, tiled=True)
    mine = full[:, :width]
    other = partner(mine, "seq", 1)
    first = upper == 0
    whole = jnp.concatenate(
        [jnp.where(first, mine, other), jnp.where(first, other, mine)], axis=1
    )
    return whole, full[:, width:]


def halve(values, axis, bit, dim):
    upper = (lax.axis_index(axis) // bit) & 1
    kept = half_of(values, upper, dim)
    got = partner(half_of(values, 1 - upper, dim), axis, bit)
    return (kept.astype(jnp.float32) + got.astype(jnp.float32)).astype(jnp.bfloat16)


def plane_steps():
    seq_bits = [("seq", 1 << i) for i in range(lax.axis_size("seq").bit_length() - 1)]
    replica_bits = [("replica", 1 << i) for i in range(lax.axis_size("replica").bit_length() - 1)]
    return seq_bits[:1], seq_bits[1:], replica_bits


def reduce_to_owner(values, dim, seq_first):
    shards = lax.axis_size("fsdp")
    values = values.astype(jnp.bfloat16)
    values = values.reshape((shards, values.shape[0] // shards) + values.shape[1:])
    cut = 2 if dim == 1 else 1
    first, rest, replicas = plane_steps()
    steps = first + (rest + replicas if seq_first else replicas + rest)
    for axis, bit in steps:
        values = halve(values, axis, bit, cut)
    values = lax.psum_scatter(values, "fsdp", scatter_dimension=0, tiled=False)
    return values, steps


def collect(values, steps, dim):
    for axis, bit in reversed(steps):
        upper = (lax.axis_index(axis) // bit) & 1
        other = partner(values, axis, bit)
        first = upper == 0
        values = jnp.concatenate(
            [jnp.where(first, values, other), jnp.where(first, other, values)], axis=dim
        )
    return values


def owner_sum(values, dim, seq_first):
    part, steps = reduce_to_owner(values, dim, seq_first)
    return collect(part, steps, dim).astype(jnp.float32)


def body(
    inputs,
    segments,
    cotangent,
    w_rows,
    m_rows,
    v_rows,
    w_down,
    m_down,
    v_down,
    smalls,
    m_small,
    v_small,
):
    seq_count, piece_rows, model_width = inputs.shape
    query_key_value_boundary = 3 * model_width
    small_rows = smalls.shape[0]

    def over_tokens(values):
        return jnp.sum(values, axis=(0, 1))

    rows_b = w_rows.astype(jnp.bfloat16)
    small_pad = jnp.pad(smalls.astype(jnp.bfloat16).T, ((0, 0), (0, LANES - small_rows)))
    matrix_qkv, small_full = gather_columns(rows_b[:, :query_key_value_boundary], small_pad)
    rows_rest, down_b, matrix_qkv, small_full = lax.optimization_barrier(
        (
            rows_b[:, query_key_value_boundary:],
            w_down.astype(jnp.bfloat16),
            matrix_qkv,
            small_full,
        )
    )
    matrix_rest, _ = gather_columns(rows_rest)
    matrix_down, _ = gather_columns(down_b)
    matrix_out = matrix_rest[:, :model_width]
    matrix_up = matrix_rest[:, model_width:]
    small_vals = small_full[:, :small_rows].T.astype(jnp.float32)
    features = inputs.astype(jnp.float32)
    normed, norm_pull_one = jax.vjp(normalize, features, small_vals[0], small_vals[1])
    normalized_block = normed.astype(jnp.bfloat16)
    projected = jnp.einsum(
        "rxj,jw->rxw", normalized_block, matrix_qkv, preferred_element_type=jnp.float32
    )
    bias = jnp.concatenate([small_vals[2], jnp.zeros_like(small_vals[2]), small_vals[3]])
    mixed = lax.all_to_all(
        (projected + bias).astype(jnp.bfloat16), "seq", split_axis=0, concat_axis=1, tiled=True
    )
    own_count = mixed.shape[0]
    own_segments = lax.dynamic_slice_in_dim(
        segments, lax.axis_index("seq") * own_count, own_count, 0
    )
    segment_rows = own_segments[:, None, :]
    segment_cols = own_segments[:, :, None]
    attended_block = lax.all_to_all(
        attend(mixed, segment_rows, segment_cols), "seq", split_axis=1, concat_axis=0, tiled=True
    )
    residual = features + (
        jnp.einsum(
            "rxj,jw->rxw",
            attended_block,
            matrix_out,
            preferred_element_type=jnp.float32,
        )
        + small_vals[4]
    )
    normed_two, norm_pull_two = jax.vjp(normalize, residual, small_vals[5], small_vals[6])
    second_normalized_block = normed_two.astype(jnp.bfloat16)
    hidden = jnp.einsum(
        "tyr,rw->tyw",
        second_normalized_block,
        matrix_up,
        preferred_element_type=jnp.float32,
    ) + small_vals[8:].reshape(-1)
    active, gelu_pull = jax.vjp(smooth_gelu, hidden)
    active_block = active.astype(jnp.bfloat16)
    activations = (
        residual
        + (
            jnp.einsum(
                "crx,xo->cro",
                active_block,
                matrix_down,
                preferred_element_type=jnp.float32,
            )
            + small_vals[7]
        )
    ).astype(jnp.bfloat16)
    upstream = cotangent.astype(jnp.float32)
    down_weight_gradient = jnp.einsum(
        "ezg,ezv->gv", active_block, cotangent, preferred_element_type=jnp.float32
    )
    grad_active = jnp.einsum(
        "tuy,qy->tuq", cotangent, matrix_down, preferred_element_type=jnp.float32
    )
    grad_hidden = gelu_pull(grad_active)[0]
    hidden_block_gradient = grad_hidden.astype(jnp.bfloat16)
    grad_up = jnp.einsum(
        "zng,znw->gw",
        second_normalized_block,
        hidden_block_gradient,
        preferred_element_type=jnp.float32,
    )
    grad_normed_two = jnp.einsum(
        "naz,ez->nae",
        hidden_block_gradient,
        matrix_up,
        preferred_element_type=jnp.float32,
    )
    grad_residual_norm, grad_gain_two, grad_shift_two = norm_pull_two(grad_normed_two)
    grad_residual = upstream + grad_residual_norm
    residual_block_gradient = grad_residual.astype(jnp.bfloat16)
    grad_out_proj = jnp.einsum(
        "azk,azx->kx", attended_block, residual_block_gradient, preferred_element_type=jnp.float32
    )
    grad_attended_b = jnp.einsum(
        "wri,yi->wry",
        residual_block_gradient,
        matrix_out,
        preferred_element_type=jnp.float32,
    ).astype(jnp.bfloat16)
    grad_attended_b, grad_up, down_weight_gradient = lax.optimization_barrier(
        (
            grad_attended_b,
            grad_up.astype(jnp.bfloat16),
            down_weight_gradient.astype(jnp.bfloat16),
        )
    )
    total_up = owner_sum(grad_up, 1, True)
    total_down = owner_sum(down_weight_gradient, 0, False)
    grad_mixed = attend_back(
        mixed,
        lax.all_to_all(grad_attended_b, "seq", split_axis=0, concat_axis=1, tiled=True),
        segment_rows,
        segment_cols,
    )
    mixed_block_gradient = lax.all_to_all(
        jnp.concatenate(grad_mixed, axis=-1), "seq", split_axis=1, concat_axis=0, tiled=True
    )
    mixed_sums = over_tokens(mixed_block_gradient.astype(jnp.float32))
    query_key_value_gradient = jnp.einsum(
        "azk,azx->kx", normalized_block, mixed_block_gradient, preferred_element_type=jnp.float32
    )
    grad_normed = jnp.einsum(
        "wri,yi->wry",
        mixed_block_gradient,
        matrix_qkv,
        preferred_element_type=jnp.float32,
    )
    grad_features, grad_gain_one, grad_shift_one = norm_pull_one(grad_normed)
    input_grad = grad_residual + grad_features
    small_head = jnp.stack(
        [
            grad_gain_one,
            grad_shift_one,
            mixed_sums[:model_width],
            mixed_sums[2 * model_width :],
            over_tokens(grad_residual),
            grad_gain_two,
            grad_shift_two,
            over_tokens(upstream),
        ]
    )
    grad_small = jnp.concatenate(
        [small_head, over_tokens(grad_hidden).reshape(-1, model_width)], axis=0
    )
    grad_mixing = jnp.concatenate([query_key_value_gradient, grad_out_proj], axis=1)
    middle = grad_mixing.shape[1] // 2
    total_rows = jnp.concatenate(
        [
            owner_sum(grad_mixing[:, :middle], 1, True),
            owner_sum(grad_mixing[:, middle:], 1, False),
            total_up,
        ],
        axis=1,
    )
    small_width = smalls.shape[1]
    total_small = lax.dynamic_slice_in_dim(
        lax.psum(grad_small, ("seq", "replica", "fsdp")),
        lax.axis_index("fsdp") * small_width,
        small_width,
        1,
    )
    new_rows, moment_rows, second_rows = adam_update(
        w_rows, m_rows, v_rows, total_rows, rate_rows, weight_decay
    )
    new_down, moment_down, second_down = adam_update(
        w_down, m_down, v_down, total_down, rate_down, weight_decay
    )
    new_small, moment_small, second_small = adam_update(
        smalls, m_small, v_small, total_small, rate_small, 0.0
    )
    return (
        activations,
        input_grad,
        new_rows,
        moment_rows,
        second_rows,
        new_down,
        moment_down,
        second_down,
        new_small,
        moment_small,
        second_small,
    )


def solution(mesh):
    in_specs = (
        P(("fsdp", "replica"), "seq", None),
        P(("fsdp", "replica"), None),
        P(("fsdp", "replica"), "seq", None),
        P("fsdp", None),
        P("fsdp", None),
        P("fsdp", None),
        P("fsdp", None),
        P("fsdp", None),
        P("fsdp", None),
        P(None, "fsdp"),
        P(None, "fsdp"),
        P(None, "fsdp"),
    )
    out_specs = (
        P(("fsdp", "replica"), "seq", None),
        P(("fsdp", "replica"), "seq", None),
        P("fsdp", None),
        P("fsdp", None),
        P("fsdp", None),
        P("fsdp", None),
        P("fsdp", None),
        P("fsdp", None),
        P(None, "fsdp"),
        P(None, "fsdp"),
        P(None, "fsdp"),
    )
    return jax.shard_map(body, mesh=mesh, in_specs=in_specs, out_specs=out_specs, check_vma=False)
```

```python
import functools

import jax
import jax.numpy as jnp
from jax import lax
from jax.experimental import pallas as pl
from jax.experimental.pallas import tpu as pltpu
from jax.sharding import PartitionSpec as P

H = 12
STEP = 10


epsilon = 1e-05
beta_first = 0.9
beta_second = 0.999
adam_epsilon = 1e-08
weight_decay = 0.1
rate_rows = 0.08
rate_down = 0.04
rate_small = 0.5
masked_score = -1e30


def normalize(values, norm_gain, norm_shift):
    centered = values - jnp.mean(values, axis=-1, keepdims=True)
    spread = jnp.mean(centered * centered, axis=-1, keepdims=True)
    return centered * lax.rsqrt(spread + epsilon) * norm_gain + norm_shift


def smooth_gelu(values):
    return jax.nn.gelu(values, approximate=True)


def adam_update(weight, moment, second, gradient, step_rate, decay_rate):
    moment_new = beta_first * moment + (1.0 - beta_first) * gradient
    second_new = beta_second * second + (1.0 - beta_second) * gradient * gradient
    moment_hat = moment_new / (1.0 - beta_first**STEP)
    second_hat = second_new / (1.0 - beta_second**STEP)
    weight_new = weight - step_rate * (
        moment_hat / (jnp.sqrt(second_hat) + adam_epsilon) + decay_rate * weight
    )
    return (weight_new, moment_new, second_new)


LANES = 128
BLOCK = 256


def lane_masks(head_width):
    lane = lax.broadcasted_iota(jnp.int32, (1, LANES), 1)
    return [
        ((lane >= start) & (lane < start + head_width)).astype(jnp.float32).astype(jnp.bfloat16)
        for start in range(0, LANES, head_width)
    ]


def transposed(values):
    return values.astype(jnp.float32).T.astype(jnp.bfloat16)


def dot_lanes(left, right):
    return lax.dot_general(
        left, right, (((1,), (1,)), ((), ())), preferred_element_type=jnp.float32
    )


def dot_plain(left, right):
    return jnp.dot(left, right, preferred_element_type=jnp.float32)


def mask_bias(places_col, places_row, start, stop):
    key_segments = places_col[:stop]
    query_segments = places_row[:, start:stop]
    key_places = lax.broadcasted_iota(jnp.int32, (stop, stop - start), 0)
    query_places = start + lax.broadcasted_iota(jnp.int32, (stop, stop - start), 1)
    allowed = (key_segments == query_segments) & (key_places <= query_places)
    return jnp.where(allowed, 0.0, masked_score)


def attend_kernel(head_width, q_ref, k_ref, v_ref, row_ref, col_ref, out_ref):
    length = q_ref.shape[1]
    keys = k_ref[0]
    values_t = transposed(v_ref[0])
    masks = lane_masks(head_width)
    scale = head_width ** (-0.5)
    for start in range(0, length, BLOCK):
        stop = start + BLOCK
        bias = mask_bias(col_ref[0], row_ref[0], start, stop)
        queries = q_ref[0, start:stop, :] * jnp.bfloat16(scale)
        parts = []
        for head, mask in enumerate(masks):
            scores = dot_lanes(keys[:stop], queries * mask) + bias
            largest = jnp.max(scores, axis=0, keepdims=True)
            weights = jnp.exp(scores - largest)
            totals = jnp.sum(weights, axis=0, keepdims=True)
            low = head * head_width
            mixed = dot_plain(
                values_t[low : low + head_width, :stop], weights.astype(jnp.bfloat16)
            )
            parts.append(mixed / totals)
        out_ref[0, start:stop, :] = jnp.concatenate(parts, axis=0).T.astype(jnp.bfloat16)


def attend_back_kernel(
    head_width, q_ref, k_ref, v_ref, g_ref, row_ref, col_ref, dq_ref, dk_ref, dv_ref, dk_sum, dv_sum
):
    length = q_ref.shape[1]
    keys = k_ref[0]
    values = v_ref[0]
    keys_t = transposed(keys)
    masks = lane_masks(head_width)
    scale = head_width ** (-0.5)
    dk_sum[...] = jnp.zeros_like(dk_sum)
    dv_sum[...] = jnp.zeros_like(dv_sum)
    for start in range(0, length, BLOCK):
        stop = start + BLOCK
        bias = mask_bias(col_ref[0], row_ref[0], start, stop)
        queries = q_ref[0, start:stop, :] * jnp.bfloat16(scale)
        grads = g_ref[0, start:stop, :]
        dq_parts, probs_parts, ds_parts = [], [], []
        query_heads = [queries * mask for mask in masks]
        grad_heads = [grads * mask for mask in masks]
        for head in range(len(masks)):
            scores = dot_lanes(keys[:stop], query_heads[head]) + bias
            largest = jnp.max(scores, axis=0, keepdims=True)
            weights = jnp.exp(scores - largest)
            totals = jnp.sum(weights, axis=0, keepdims=True)
            probs = weights * (1.0 / totals)
            grad_probs = dot_lanes(values[:stop], grad_heads[head])
            centered = jnp.sum(probs * grad_probs, axis=0, keepdims=True)
            grad_scores = (probs * (grad_probs - centered)).astype(jnp.bfloat16)
            low = head * head_width
            dq_parts.append(dot_plain(keys_t[low : low + head_width, :stop], grad_scores))
            ds_parts.append(grad_scores)
            probs_parts.append(probs.astype(jnp.bfloat16))
        dk_sum[:stop, :] += dot_plain(
            jnp.concatenate(ds_parts, axis=1), jnp.concatenate(query_heads, axis=0)
        )
        dv_sum[:stop, :] += dot_plain(
            jnp.concatenate(probs_parts, axis=1), jnp.concatenate(grad_heads, axis=0)
        )
        dq = jnp.concatenate(dq_parts, axis=0) * scale
        dq_ref[0, start:stop, :] = dq.T.astype(jnp.bfloat16)
    dk_ref[0] = dk_sum[...].astype(jnp.bfloat16)
    dv_ref[0] = dv_sum[...].astype(jnp.bfloat16)


def attention_specs(length, groups):
    def column(offset):
        return pl.BlockSpec((1, length, LANES), lambda n, j: (n, 0, offset * groups + j))

    row = pl.BlockSpec((1, 1, length), lambda n, j: (n, 0, 0))
    col = pl.BlockSpec((1, length, 1), lambda n, j: (n, 0, 0))
    return column, row, col


def attend(mixed, rows, cols):
    count, length, width = mixed.shape
    width //= 3
    groups = width // LANES
    column, row, col = attention_specs(length, groups)
    return pl.pallas_call(
        functools.partial(attend_kernel, width // H),
        grid=(count, groups),
        in_specs=[column(0), column(1), column(2), row, col],
        out_specs=column(0),
        out_shape=jax.ShapeDtypeStruct((count, length, width), jnp.bfloat16),
        compiler_params=pltpu.CompilerParams(vmem_limit_bytes=48 * 2**20),
        cost_estimate=pl.CostEstimate(
            flops=3 * count * length * length * width,
            bytes_accessed=8 * count * length * width,
            transcendentals=count * H * length * length // 2,
        ),
    )(mixed, mixed, mixed, rows, cols)


def attend_back(mixed, grads, rows, cols):
    count, length, width = grads.shape
    groups = width // LANES
    column, row, col = attention_specs(length, groups)
    shape = jax.ShapeDtypeStruct((count, length, width), jnp.bfloat16)
    return pl.pallas_call(
        functools.partial(attend_back_kernel, width // H),
        grid=(count, groups),
        in_specs=[column(0), column(1), column(2), column(0), row, col],
        out_specs=[column(0)] * 3,
        out_shape=[shape] * 3,
        scratch_shapes=[pltpu.VMEM((length, LANES), jnp.float32)] * 2,
        compiler_params=pltpu.CompilerParams(vmem_limit_bytes=48 * 2**20),
        cost_estimate=pl.CostEstimate(
            flops=7 * count * length * length * width,
            bytes_accessed=14 * count * length * width,
            transcendentals=count * H * length * length // 2,
        ),
    )(mixed, mixed, mixed, grads, rows, cols)


def partner(values, axis, bit):
    size = lax.axis_size(axis)
    return lax.ppermute(values, axis, [(i, i ^ bit) for i in range(size)])


def half_of(values, upper, dim):
    half = values.shape[dim] // 2
    return lax.dynamic_slice_in_dim(values, upper * half, half, dim)


def gather_half(values):
    return lax.all_gather(
        half_of(values, lax.axis_index("seq") & 1, 1), "fsdp", axis=0, tiled=True
    )


def swap_halves(mine):
    other = partner(mine, "seq", 1)
    first = lax.axis_index("seq") & 1 == 0
    return jnp.concatenate(
        [jnp.where(first, mine, other), jnp.where(first, other, mine)], axis=1
    )


def to_sequences(values):
    size = lax.axis_size("seq")
    count, piece, width = values.shape
    values = lax.all_to_all(values, "seq", split_axis=0, concat_axis=0, tiled=True)
    values = jnp.moveaxis(values.reshape(size, count // size, piece, width), 0, 1)
    return values.reshape(count // size, size * piece, width)


def to_pieces(values):
    size = lax.axis_size("seq")
    count, length, width = values.shape
    values = jnp.moveaxis(values.reshape(count, size, length // size, width), 1, 0)
    values = values.reshape(size * count, length // size, width)
    return lax.all_to_all(values, "seq", split_axis=0, concat_axis=0, tiled=True)


def butterfly_sum(values, axes):
    for axis in axes:
        for bit in range(lax.axis_size(axis).bit_length() - 1):
            values = values + partner(values, axis, 1 << bit)
    return values


def halve(values, axis, bit, dim):
    upper = (lax.axis_index(axis) // bit) & 1
    kept = half_of(values, upper, dim)
    got = partner(half_of(values, 1 - upper, dim), axis, bit)
    return (kept.astype(jnp.float32) + got.astype(jnp.float32)).astype(jnp.bfloat16)


def plane_steps():
    seq_bits = [("seq", 1 << i) for i in range(lax.axis_size("seq").bit_length() - 1)]
    replica_bits = [("replica", 1 << i) for i in range(lax.axis_size("replica").bit_length() - 1)]
    return seq_bits[:1], seq_bits[1:], replica_bits


def by_owner(values):
    shards = lax.axis_size("fsdp")
    values = values.astype(jnp.bfloat16)
    return values.reshape((shards, values.shape[0] // shards) + values.shape[1:])


def halve_all(values, steps, cut):
    for axis, bit in steps:
        values = halve(values, axis, bit, cut)
    return values


def scatter_rows(values):
    return lax.psum_scatter(values, "fsdp", scatter_dimension=0, tiled=False)


def collect(values, steps, dim):
    for axis, bit in reversed(steps):
        upper = (lax.axis_index(axis) // bit) & 1
        other = partner(values, axis, bit)
        first = upper == 0
        values = jnp.concatenate(
            [jnp.where(first, values, other), jnp.where(first, other, values)], axis=dim
        )
    return values


def body(
    inputs,
    segments,
    cotangent,
    w_rows,
    m_rows,
    v_rows,
    w_down,
    m_down,
    v_down,
    smalls,
    m_small,
    v_small,
):
    seq_count, piece_rows, model_width = inputs.shape
    query_key_value_boundary = 3 * model_width
    small_rows = smalls.shape[0]

    def over_tokens(values):
        return jnp.sum(values, axis=(0, 1))

    rows_b = w_rows.astype(jnp.bfloat16)
    small_pad = jnp.pad(smalls.astype(jnp.bfloat16).T, ((0, 0), (0, LANES - small_rows)))
    own_qkv = half_of(rows_b[:, :query_key_value_boundary], lax.axis_index("seq") & 1, 1)
    half_width = own_qkv.shape[1]
    full_qkv = lax.all_gather(
        jnp.concatenate([own_qkv, small_pad], axis=1), "fsdp", axis=0, tiled=True
    )
    rows_rest, down_b, full_qkv = lax.optimization_barrier(
        (rows_b[:, query_key_value_boundary:], w_down.astype(jnp.bfloat16), full_qkv)
    )
    half_rest = gather_half(rows_rest)
    half_down = gather_half(down_b)
    matrix_qkv = swap_halves(full_qkv[:, :half_width])
    small_full = full_qkv[:, half_width:]
    small_vals = small_full[:, :small_rows].T.astype(jnp.float32)
    features = inputs.astype(jnp.float32)
    normed, norm_pull_one = jax.vjp(normalize, features, small_vals[0], small_vals[1])
    normalized_block = normed.astype(jnp.bfloat16)
    projected = jnp.einsum(
        "rxj,jw->rxw", normalized_block, matrix_qkv, preferred_element_type=jnp.float32
    )
    bias = jnp.concatenate([small_vals[2], jnp.zeros_like(small_vals[2]), small_vals[3]])
    mixed = to_sequences((projected + bias).astype(jnp.bfloat16))
    own_count = mixed.shape[0]
    own_segments = lax.dynamic_slice_in_dim(
        segments, lax.axis_index("seq") * own_count, own_count, 0
    )
    segment_rows = own_segments[:, None, :]
    segment_cols = own_segments[:, :, None]
    attended_own, half_rest, half_down = lax.optimization_barrier(
        (attend(mixed, segment_rows, segment_cols), half_rest, half_down)
    )
    attended_block = to_pieces(attended_own)
    matrix_rest = swap_halves(half_rest)
    matrix_down = swap_halves(half_down)
    matrix_out = matrix_rest[:, :model_width]
    matrix_up = matrix_rest[:, model_width:]
    residual = features + (
        jnp.einsum(
            "rxj,jw->rxw",
            attended_block,
            matrix_out,
            preferred_element_type=jnp.float32,
        )
        + small_vals[4]
    )
    normed_two, norm_pull_two = jax.vjp(normalize, residual, small_vals[5], small_vals[6])
    second_normalized_block = normed_two.astype(jnp.bfloat16)
    hidden = jnp.einsum(
        "tyr,rw->tyw",
        second_normalized_block,
        matrix_up,
        preferred_element_type=jnp.float32,
    ) + small_vals[8:].reshape(-1)
    active, gelu_pull = jax.vjp(smooth_gelu, hidden)
    active_block = active.astype(jnp.bfloat16)
    activations = (
        residual
        + (
            jnp.einsum(
                "crx,xo->cro",
                active_block,
                matrix_down,
                preferred_element_type=jnp.float32,
            )
            + small_vals[7]
        )
    ).astype(jnp.bfloat16)
    upstream = cotangent.astype(jnp.float32)
    down_weight_gradient = jnp.einsum(
        "ezg,ezv->gv", active_block, cotangent, preferred_element_type=jnp.float32
    )
    grad_active = jnp.einsum(
        "tuy,qy->tuq", cotangent, matrix_down, preferred_element_type=jnp.float32
    )
    grad_hidden = gelu_pull(grad_active)[0]
    hidden_block_gradient = grad_hidden.astype(jnp.bfloat16)
    grad_up = jnp.einsum(
        "zng,znw->gw",
        second_normalized_block,
        hidden_block_gradient,
        preferred_element_type=jnp.float32,
    )
    grad_normed_two = jnp.einsum(
        "naz,ez->nae",
        hidden_block_gradient,
        matrix_up,
        preferred_element_type=jnp.float32,
    )
    grad_residual_norm, grad_gain_two, grad_shift_two = norm_pull_two(grad_normed_two)
    grad_residual = upstream + grad_residual_norm
    residual_block_gradient = grad_residual.astype(jnp.bfloat16)
    grad_out_proj = jnp.einsum(
        "azk,azx->kx", attended_block, residual_block_gradient, preferred_element_type=jnp.float32
    )
    grad_attended_b = jnp.einsum(
        "wri,yi->wry",
        residual_block_gradient,
        matrix_out,
        preferred_element_type=jnp.float32,
    ).astype(jnp.bfloat16)
    grad_attended_b, grad_up, down_weight_gradient = lax.optimization_barrier(
        (
            grad_attended_b,
            grad_up.astype(jnp.bfloat16),
            down_weight_gradient.astype(jnp.bfloat16),
        )
    )
    first, rest, replicas = plane_steps()
    part_up = halve_all(by_owner(grad_up), first, 2)
    part_down = halve_all(by_owner(down_weight_gradient), first, 1)
    grad_attended_own, part_up, part_down = lax.optimization_barrier(
        (to_sequences(grad_attended_b), part_up, part_down)
    )
    part_up = halve_all(part_up, rest + replicas, 2)
    part_down = halve_all(part_down, replicas + rest, 1)
    up_columns = part_up.shape[2]
    part_down = jnp.concatenate(
        [part_down[:, :, :up_columns], part_down[:, :, up_columns:]], axis=1
    )
    owned = scatter_rows(jnp.concatenate([part_up, part_down], axis=2))
    total_up = collect(owned[:, :up_columns], first + rest + replicas, 1)
    owned_down = owned[:, up_columns:]
    down_rows = owned_down.shape[0] // 2
    total_down = collect(
        jnp.concatenate([owned_down[:down_rows], owned_down[down_rows:]], axis=1),
        first + replicas + rest,
        0,
    ).astype(jnp.float32)
    grad_mixed = attend_back(mixed, grad_attended_own, segment_rows, segment_cols)
    mixed_block_gradient = to_pieces(jnp.concatenate(grad_mixed, axis=-1))
    mixed_sums = over_tokens(mixed_block_gradient.astype(jnp.float32))
    query_key_value_gradient = jnp.einsum(
        "azk,azx->kx", normalized_block, mixed_block_gradient, preferred_element_type=jnp.float32
    )
    grad_normed = jnp.einsum(
        "wri,yi->wry",
        mixed_block_gradient,
        matrix_qkv,
        preferred_element_type=jnp.float32,
    )
    grad_features, grad_gain_one, grad_shift_one = norm_pull_one(grad_normed)
    input_grad = grad_residual + grad_features
    small_head = jnp.stack(
        [
            grad_gain_one,
            grad_shift_one,
            mixed_sums[:model_width],
            mixed_sums[2 * model_width :],
            over_tokens(grad_residual),
            grad_gain_two,
            grad_shift_two,
            over_tokens(upstream),
        ]
    )
    grad_small = jnp.concatenate(
        [small_head, over_tokens(grad_hidden).reshape(-1, model_width)], axis=0
    )
    grad_mixing = jnp.concatenate([query_key_value_gradient, grad_out_proj], axis=1)
    middle = grad_mixing.shape[1] // 2
    part_left = halve_all(by_owner(grad_mixing[:, :middle]), first + rest + replicas, 2)
    part_right = halve_all(by_owner(grad_mixing[:, middle:]), first + replicas + rest, 2)
    left_columns = part_left.shape[2]
    owned = scatter_rows(jnp.concatenate([part_left, part_right], axis=2))
    total_rows = jnp.concatenate(
        [
            collect(owned[:, :left_columns], first + rest + replicas, 1),
            collect(owned[:, left_columns:], first + replicas + rest, 1),
            total_up,
        ],
        axis=1,
    ).astype(jnp.float32)
    small_width = smalls.shape[1]
    total_small = lax.dynamic_slice_in_dim(
        butterfly_sum(grad_small, ("seq", "replica", "fsdp")),
        lax.axis_index("fsdp") * small_width,
        small_width,
        1,
    )
    new_rows, moment_rows, second_rows = adam_update(
        w_rows, m_rows, v_rows, total_rows, rate_rows, weight_decay
    )
    new_down, moment_down, second_down = adam_update(
        w_down, m_down, v_down, total_down, rate_down, weight_decay
    )
    new_small, moment_small, second_small = adam_update(
        smalls, m_small, v_small, total_small, rate_small, 0.0
    )
    return (
        activations,
        input_grad,
        new_rows,
        moment_rows,
        second_rows,
        new_down,
        moment_down,
        second_down,
        new_small,
        moment_small,
        second_small,
    )


def solution(mesh):
    in_specs = (
        P(("fsdp", "replica"), "seq", None),
        P(("fsdp", "replica"), None),
        P(("fsdp", "replica"), "seq", None),
        P("fsdp", None),
        P("fsdp", None),
        P("fsdp", None),
        P("fsdp", None),
        P("fsdp", None),
        P("fsdp", None),
        P(None, "fsdp"),
        P(None, "fsdp"),
        P(None, "fsdp"),
    )
    out_specs = (
        P(("fsdp", "replica"), "seq", None),
        P(("fsdp", "replica"), "seq", None),
        P("fsdp", None),
        P("fsdp", None),
        P("fsdp", None),
        P("fsdp", None),
        P("fsdp", None),
        P("fsdp", None),
        P(None, "fsdp"),
        P(None, "fsdp"),
        P(None, "fsdp"),
    )
    return jax.shard_map(body, mesh=mesh, in_specs=in_specs, out_specs=out_specs, check_vma=False)
```

```python
import functools

import jax
import jax.numpy as jnp
from jax import lax
from jax.experimental import pallas as pl
from jax.experimental.pallas import tpu as pltpu
from jax.sharding import PartitionSpec as P

H = 12
STEP = 10


epsilon = 1e-05
beta_first = 0.9
beta_second = 0.999
adam_epsilon = 1e-08
weight_decay = 0.1
rate_rows = 0.08
rate_down = 0.04
rate_small = 0.5
masked_score = -1e30


def normalize(values, norm_gain, norm_shift):
    centered = values - jnp.mean(values, axis=-1, keepdims=True)
    spread = jnp.mean(centered * centered, axis=-1, keepdims=True)
    return centered * lax.rsqrt(spread + epsilon) * norm_gain + norm_shift


def smooth_gelu(values):
    return jax.nn.gelu(values, approximate=True)


def adam_update(weight, moment, second, gradient, step_rate, decay_rate):
    moment_new = beta_first * moment + (1.0 - beta_first) * gradient
    second_new = beta_second * second + (1.0 - beta_second) * gradient * gradient
    moment_hat = moment_new / (1.0 - beta_first**STEP)
    second_hat = second_new / (1.0 - beta_second**STEP)
    weight_new = weight - step_rate * (
        moment_hat / (jnp.sqrt(second_hat) + adam_epsilon) + decay_rate * weight
    )
    return (weight_new, moment_new, second_new)


LANES = 128
BLOCK = 256


def lane_masks(head_width):
    lane = lax.broadcasted_iota(jnp.int32, (1, LANES), 1)
    return [
        ((lane >= start) & (lane < start + head_width)).astype(jnp.float32).astype(jnp.bfloat16)
        for start in range(0, LANES, head_width)
    ]


def transposed(values):
    return values.astype(jnp.float32).T.astype(jnp.bfloat16)


def dot_lanes(left, right):
    return lax.dot_general(
        left, right, (((1,), (1,)), ((), ())), preferred_element_type=jnp.float32
    )


def dot_plain(left, right):
    return jnp.dot(left, right, preferred_element_type=jnp.float32)


def mask_bias(places_col, places_row, start, stop):
    key_segments = places_col[:stop]
    query_segments = places_row[:, start:stop]
    key_places = lax.broadcasted_iota(jnp.int32, (stop, stop - start), 0)
    query_places = start + lax.broadcasted_iota(jnp.int32, (stop, stop - start), 1)
    allowed = (key_segments == query_segments) & (key_places <= query_places)
    return jnp.where(allowed, 0.0, masked_score)


def attend_kernel(head_width, q_ref, k_ref, v_ref, row_ref, col_ref, out_ref):
    length = q_ref.shape[1]
    keys = k_ref[0]
    values_t = transposed(v_ref[0])
    masks = lane_masks(head_width)
    scale = head_width ** (-0.5)
    for start in range(0, length, BLOCK):
        stop = start + BLOCK
        bias = mask_bias(col_ref[0], row_ref[0], start, stop)
        queries = q_ref[0, start:stop, :] * jnp.bfloat16(scale)
        parts = []
        for head, mask in enumerate(masks):
            scores = dot_lanes(keys[:stop], queries * mask) + bias
            largest = jnp.max(scores, axis=0, keepdims=True)
            weights = jnp.exp(scores - largest)
            totals = jnp.sum(weights, axis=0, keepdims=True)
            low = head * head_width
            mixed = dot_plain(
                values_t[low : low + head_width, :stop], weights.astype(jnp.bfloat16)
            )
            parts.append(mixed / totals)
        out_ref[0, start:stop, :] = jnp.concatenate(parts, axis=0).T.astype(jnp.bfloat16)


def attend_back_kernel(
    head_width, q_ref, k_ref, v_ref, g_ref, row_ref, col_ref, dq_ref, dk_ref, dv_ref, dk_sum, dv_sum
):
    length = q_ref.shape[1]
    keys = k_ref[0]
    values = v_ref[0]
    keys_t = transposed(keys)
    masks = lane_masks(head_width)
    scale = head_width ** (-0.5)
    dk_sum[...] = jnp.zeros_like(dk_sum)
    dv_sum[...] = jnp.zeros_like(dv_sum)
    for start in range(0, length, BLOCK):
        stop = start + BLOCK
        bias = mask_bias(col_ref[0], row_ref[0], start, stop)
        queries = q_ref[0, start:stop, :] * jnp.bfloat16(scale)
        grads = g_ref[0, start:stop, :]
        dq_parts, probs_parts, ds_parts = [], [], []
        query_heads = [queries * mask for mask in masks]
        grad_heads = [grads * mask for mask in masks]
        for head in range(len(masks)):
            scores = dot_lanes(keys[:stop], query_heads[head]) + bias
            largest = jnp.max(scores, axis=0, keepdims=True)
            weights = jnp.exp(scores - largest)
            totals = jnp.sum(weights, axis=0, keepdims=True)
            probs = weights * (1.0 / totals)
            grad_probs = dot_lanes(values[:stop], grad_heads[head])
            centered = jnp.sum(probs * grad_probs, axis=0, keepdims=True)
            grad_scores = (probs * (grad_probs - centered)).astype(jnp.bfloat16)
            low = head * head_width
            dq_parts.append(dot_plain(keys_t[low : low + head_width, :stop], grad_scores))
            ds_parts.append(grad_scores)
            probs_parts.append(probs.astype(jnp.bfloat16))
        dk_sum[:stop, :] += dot_plain(
            jnp.concatenate(ds_parts, axis=1), jnp.concatenate(query_heads, axis=0)
        )
        dv_sum[:stop, :] += dot_plain(
            jnp.concatenate(probs_parts, axis=1), jnp.concatenate(grad_heads, axis=0)
        )
        dq = jnp.concatenate(dq_parts, axis=0) * scale
        dq_ref[0, start:stop, :] = dq.T.astype(jnp.bfloat16)
    dk_ref[0] = dk_sum[...].astype(jnp.bfloat16)
    dv_ref[0] = dv_sum[...].astype(jnp.bfloat16)


def attention_specs(length, groups):
    def column(offset):
        return pl.BlockSpec((1, length, LANES), lambda n, j: (n, 0, offset * groups + j))

    row = pl.BlockSpec((1, 1, length), lambda n, j: (n, 0, 0))
    col = pl.BlockSpec((1, length, 1), lambda n, j: (n, 0, 0))
    return column, row, col


def attend(mixed, rows, cols, head_width):
    count, length, width = mixed.shape
    width //= 3
    groups = width // LANES
    column, row, col = attention_specs(length, groups)
    return pl.pallas_call(
        functools.partial(attend_kernel, head_width),
        grid=(count, groups),
        in_specs=[column(0), column(1), column(2), row, col],
        out_specs=column(0),
        out_shape=jax.ShapeDtypeStruct((count, length, width), jnp.bfloat16),
        compiler_params=pltpu.CompilerParams(vmem_limit_bytes=48 * 2**20),
        cost_estimate=pl.CostEstimate(
            flops=12 * count * length * length * width,
            bytes_accessed=8 * count * length * width,
            transcendentals=count * (width // head_width) * length * length // 2,
        ),
    )(mixed, mixed, mixed, rows, cols)


def attend_back(mixed, grads, rows, cols, head_width):
    count, length, width = grads.shape
    groups = width // LANES
    column, row, col = attention_specs(length, groups)
    shape = jax.ShapeDtypeStruct((count, length, width), jnp.bfloat16)
    return pl.pallas_call(
        functools.partial(attend_back_kernel, head_width),
        grid=(count, groups),
        in_specs=[column(0), column(1), column(2), column(0), row, col],
        out_specs=[column(0)] * 3,
        out_shape=[shape] * 3,
        scratch_shapes=[pltpu.VMEM((length, LANES), jnp.float32)] * 2,
        compiler_params=pltpu.CompilerParams(vmem_limit_bytes=48 * 2**20),
        cost_estimate=pl.CostEstimate(
            flops=40 * count * length * length * width,
            bytes_accessed=14 * count * length * width,
            transcendentals=count * (width // head_width) * length * length // 2,
        ),
    )(mixed, mixed, mixed, grads, rows, cols)


def partner(values, axis, bit):
    size = lax.axis_size(axis)
    return lax.ppermute(values, axis, [(i, i ^ bit) for i in range(size)])


def half_of(values, upper, dim):
    half = values.shape[dim] // 2
    return lax.dynamic_slice_in_dim(values, upper * half, half, dim)


def gather_half(values):
    return lax.all_gather(
        half_of(values, lax.axis_index("seq") & 1, 1), "fsdp", axis=0, tiled=True
    )


def swap_halves(mine):
    other = partner(mine, "seq", 1)
    first = lax.axis_index("seq") & 1 == 0
    return jnp.concatenate(
        [jnp.where(first, mine, other), jnp.where(first, other, mine)], axis=1
    )


def to_sequences(values):
    size = lax.axis_size("seq")
    count, piece, width = values.shape
    values = lax.all_to_all(values, "seq", split_axis=0, concat_axis=0, tiled=True)
    values = jnp.moveaxis(values.reshape(size, count // size, piece, width), 0, 1)
    return values.reshape(count // size, size * piece, width)


def to_pieces(values):
    size = lax.axis_size("seq")
    count, length, width = values.shape
    values = jnp.moveaxis(values.reshape(count, size, length // size, width), 1, 0)
    values = values.reshape(size * count, length // size, width)
    return lax.all_to_all(values, "seq", split_axis=0, concat_axis=0, tiled=True)


def side_by_side(parts, kinds):
    return jnp.concatenate(
        [piece for row in zip(*(jnp.split(part, kinds, axis=-1) for part in parts)) for piece in row],
        axis=-1,
    )


def butterfly_sum(values, axes):
    for axis in axes:
        for bit in range(lax.axis_size(axis).bit_length() - 1):
            values = values + partner(values, axis, 1 << bit)
    return values


def halve(values, axis, bit, dim):
    upper = (lax.axis_index(axis) // bit) & 1
    kept = half_of(values, upper, dim)
    got = partner(half_of(values, 1 - upper, dim), axis, bit)
    return (kept.astype(jnp.float32) + got.astype(jnp.float32)).astype(jnp.bfloat16)


def plane_steps():
    seq_bits = [("seq", 1 << i) for i in range(lax.axis_size("seq").bit_length() - 1)]
    replica_bits = [("replica", 1 << i) for i in range(lax.axis_size("replica").bit_length() - 1)]
    return seq_bits[:1], seq_bits[1:], replica_bits


def by_owner(values):
    shards = lax.axis_size("fsdp")
    values = values.astype(jnp.bfloat16)
    return values.reshape((shards, values.shape[0] // shards) + values.shape[1:])


def halve_all(values, steps, cut):
    for axis, bit in steps:
        values = halve(values, axis, bit, cut)
    return values


def scatter_rows(values):
    return lax.psum_scatter(values, "fsdp", scatter_dimension=0, tiled=False)


def collect(values, steps, dim):
    for axis, bit in reversed(steps):
        upper = (lax.axis_index(axis) // bit) & 1
        other = partner(values, axis, bit)
        first = upper == 0
        values = jnp.concatenate(
            [jnp.where(first, values, other), jnp.where(first, other, values)], axis=dim
        )
    return values


def body(
    inputs,
    segments,
    cotangent,
    w_rows,
    m_rows,
    v_rows,
    w_down,
    m_down,
    v_down,
    smalls,
    m_small,
    v_small,
):
    seq_count, piece_rows, model_width = inputs.shape
    query_key_value_boundary = 3 * model_width
    small_rows = smalls.shape[0]

    def over_tokens(values):
        return jnp.sum(values, axis=(0, 1))

    rows_b = w_rows.astype(jnp.bfloat16)
    small_pad = jnp.pad(smalls.astype(jnp.bfloat16).T, ((0, 0), (0, LANES - small_rows)))
    own_qkv = half_of(rows_b[:, :query_key_value_boundary], lax.axis_index("seq") & 1, 1)
    half_width = own_qkv.shape[1]
    full_qkv = lax.all_gather(
        jnp.concatenate([own_qkv, small_pad], axis=1), "fsdp", axis=0, tiled=True
    )
    rows_rest, down_b, full_qkv = lax.optimization_barrier(
        (rows_b[:, query_key_value_boundary:], w_down.astype(jnp.bfloat16), full_qkv)
    )
    half_rest = gather_half(rows_rest)
    half_down = gather_half(down_b)
    matrix_qkv = swap_halves(full_qkv[:, :half_width])
    small_full = full_qkv[:, half_width:]
    small_vals = small_full[:, :small_rows].T.astype(jnp.float32)
    features = inputs.astype(jnp.float32)
    normed, norm_pull_one = jax.vjp(normalize, features, small_vals[0], small_vals[1])
    normalized_block = normed.astype(jnp.bfloat16)
    projected = jnp.einsum(
        "rxj,jw->rxw", normalized_block, matrix_qkv, preferred_element_type=jnp.float32
    )
    bias = jnp.concatenate([small_vals[2], jnp.zeros_like(small_vals[2]), small_vals[3]])
    projected = (projected + bias).astype(jnp.bfloat16)
    head_width = model_width // H
    middle_column = model_width // 2
    halves = [slice(0, middle_column), slice(middle_column, model_width)]
    kinds = jnp.split(projected, 3, axis=-1)
    mixed = [
        to_sequences(jnp.concatenate([kind[..., half] for kind in kinds], axis=-1))
        for half in halves
    ]
    own_count = mixed[0].shape[0]
    own_segments = lax.dynamic_slice_in_dim(
        segments, lax.axis_index("seq") * own_count, own_count, 0
    )
    segment_rows = own_segments[:, None, :]
    segment_cols = own_segments[:, :, None]
    attended_first = attend(mixed[0], segment_rows, segment_cols, head_width)
    attended_first, second_mixed = lax.optimization_barrier((attended_first, mixed[1]))
    attended_second, half_rest, half_down = lax.optimization_barrier(
        (attend(second_mixed, segment_rows, segment_cols, head_width), half_rest, half_down)
    )
    attended_block = jnp.concatenate(
        [to_pieces(attended_first), to_pieces(attended_second)], axis=-1
    )
    matrix_rest = swap_halves(half_rest)
    matrix_down = swap_halves(half_down)
    matrix_out = matrix_rest[:, :model_width]
    matrix_up = matrix_rest[:, model_width:]
    residual = features + (
        jnp.einsum(
            "rxj,jw->rxw",
            attended_block,
            matrix_out,
            preferred_element_type=jnp.float32,
        )
        + small_vals[4]
    )
    normed_two, norm_pull_two = jax.vjp(normalize, residual, small_vals[5], small_vals[6])
    second_normalized_block = normed_two.astype(jnp.bfloat16)
    hidden = jnp.einsum(
        "tyr,rw->tyw",
        second_normalized_block,
        matrix_up,
        preferred_element_type=jnp.float32,
    ) + small_vals[8:].reshape(-1)
    active, gelu_pull = jax.vjp(smooth_gelu, hidden)
    active_block = active.astype(jnp.bfloat16)
    activations = (
        residual
        + (
            jnp.einsum(
                "crx,xo->cro",
                active_block,
                matrix_down,
                preferred_element_type=jnp.float32,
            )
            + small_vals[7]
        )
    ).astype(jnp.bfloat16)
    upstream = cotangent.astype(jnp.float32)
    down_weight_gradient = jnp.einsum(
        "ezg,ezv->gv", active_block, cotangent, preferred_element_type=jnp.float32
    )
    grad_active = jnp.einsum(
        "tuy,qy->tuq", cotangent, matrix_down, preferred_element_type=jnp.float32
    )
    grad_hidden = gelu_pull(grad_active)[0]
    hidden_block_gradient = grad_hidden.astype(jnp.bfloat16)
    grad_up = jnp.einsum(
        "zng,znw->gw",
        second_normalized_block,
        hidden_block_gradient,
        preferred_element_type=jnp.float32,
    )
    grad_normed_two = jnp.einsum(
        "naz,ez->nae",
        hidden_block_gradient,
        matrix_up,
        preferred_element_type=jnp.float32,
    )
    grad_residual_norm, grad_gain_two, grad_shift_two = norm_pull_two(grad_normed_two)
    grad_residual = upstream + grad_residual_norm
    residual_block_gradient = grad_residual.astype(jnp.bfloat16)
    grad_out_proj = jnp.einsum(
        "azk,azx->kx", attended_block, residual_block_gradient, preferred_element_type=jnp.float32
    )
    grad_attended_b = jnp.einsum(
        "wri,yi->wry",
        residual_block_gradient,
        matrix_out,
        preferred_element_type=jnp.float32,
    ).astype(jnp.bfloat16)
    grad_attended_b, grad_up, down_weight_gradient = lax.optimization_barrier(
        (
            grad_attended_b,
            grad_up.astype(jnp.bfloat16),
            down_weight_gradient.astype(jnp.bfloat16),
        )
    )
    first, rest, replicas = plane_steps()
    part_up = halve_all(by_owner(grad_up), first, 2)
    part_down = halve_all(by_owner(down_weight_gradient), first, 1)
    grad_first, grad_second, part_up, part_down = lax.optimization_barrier(
        (
            to_sequences(grad_attended_b[..., halves[0]]),
            to_sequences(grad_attended_b[..., halves[1]]),
            part_up,
            part_down,
        )
    )
    back_first = attend_back(mixed[0], grad_first, segment_rows, segment_cols, head_width)
    back_first, grad_second, part_up, part_down = lax.optimization_barrier(
        (
            jnp.concatenate(back_first, axis=-1),
            grad_second,
            halve_all(part_up, rest, 2),
            halve_all(part_down, replicas, 1),
        )
    )
    mixed_first = to_pieces(back_first)
    back_second = attend_back(mixed[1], grad_second, segment_rows, segment_cols, head_width)
    back_second, part_up, part_down = lax.optimization_barrier(
        (
            jnp.concatenate(back_second, axis=-1),
            halve_all(part_up, replicas, 2),
            halve_all(part_down, rest, 1),
        )
    )
    up_columns = part_up.shape[2]
    part_down = jnp.concatenate(
        [part_down[:, :, :up_columns], part_down[:, :, up_columns:]], axis=1
    )
    owned = scatter_rows(jnp.concatenate([part_up, part_down], axis=2))
    total_up = collect(owned[:, :up_columns], first + rest + replicas, 1)
    owned_down = owned[:, up_columns:]
    down_rows = owned_down.shape[0] // 2
    total_down = collect(
        jnp.concatenate([owned_down[:down_rows], owned_down[down_rows:]], axis=1),
        first + replicas + rest,
        0,
    ).astype(jnp.float32)
    mixed_block_gradient = side_by_side([mixed_first, to_pieces(back_second)], 3)
    mixed_sums = over_tokens(mixed_block_gradient.astype(jnp.float32))
    query_key_value_gradient = jnp.einsum(
        "azk,azx->kx", normalized_block, mixed_block_gradient, preferred_element_type=jnp.float32
    )
    grad_normed = jnp.einsum(
        "wri,yi->wry",
        mixed_block_gradient,
        matrix_qkv,
        preferred_element_type=jnp.float32,
    )
    grad_features, grad_gain_one, grad_shift_one = norm_pull_one(grad_normed)
    input_grad = grad_residual + grad_features
    small_head = jnp.stack(
        [
            grad_gain_one,
            grad_shift_one,
            mixed_sums[:model_width],
            mixed_sums[2 * model_width :],
            over_tokens(grad_residual),
            grad_gain_two,
            grad_shift_two,
            over_tokens(upstream),
        ]
    )
    grad_small = jnp.concatenate(
        [small_head, over_tokens(grad_hidden).reshape(-1, model_width)], axis=0
    )
    grad_mixing = jnp.concatenate([query_key_value_gradient, grad_out_proj], axis=1)
    middle = grad_mixing.shape[1] // 2
    part_left = halve_all(by_owner(grad_mixing[:, :middle]), first + rest + replicas, 2)
    part_right = halve_all(by_owner(grad_mixing[:, middle:]), first + replicas + rest, 2)
    left_columns = part_left.shape[2]
    owned = scatter_rows(jnp.concatenate([part_left, part_right], axis=2))
    total_rows = jnp.concatenate(
        [
            collect(owned[:, :left_columns], first + rest + replicas, 1),
            collect(owned[:, left_columns:], first + replicas + rest, 1),
            total_up,
        ],
        axis=1,
    ).astype(jnp.float32)
    small_width = smalls.shape[1]
    total_small = lax.dynamic_slice_in_dim(
        butterfly_sum(grad_small, ("seq", "replica", "fsdp")),
        lax.axis_index("fsdp") * small_width,
        small_width,
        1,
    )
    new_rows, moment_rows, second_rows = adam_update(
        w_rows, m_rows, v_rows, total_rows, rate_rows, weight_decay
    )
    new_down, moment_down, second_down = adam_update(
        w_down, m_down, v_down, total_down, rate_down, weight_decay
    )
    new_small, moment_small, second_small = adam_update(
        smalls, m_small, v_small, total_small, rate_small, 0.0
    )
    return (
        activations,
        input_grad,
        new_rows,
        moment_rows,
        second_rows,
        new_down,
        moment_down,
        second_down,
        new_small,
        moment_small,
        second_small,
    )


def solution(mesh):
    in_specs = (
        P(("fsdp", "replica"), "seq", None),
        P(("fsdp", "replica"), None),
        P(("fsdp", "replica"), "seq", None),
        P("fsdp", None),
        P("fsdp", None),
        P("fsdp", None),
        P("fsdp", None),
        P("fsdp", None),
        P("fsdp", None),
        P(None, "fsdp"),
        P(None, "fsdp"),
        P(None, "fsdp"),
    )
    out_specs = (
        P(("fsdp", "replica"), "seq", None),
        P(("fsdp", "replica"), "seq", None),
        P("fsdp", None),
        P("fsdp", None),
        P("fsdp", None),
        P("fsdp", None),
        P("fsdp", None),
        P("fsdp", None),
        P(None, "fsdp"),
        P(None, "fsdp"),
        P(None, "fsdp"),
    )
    return jax.shard_map(body, mesh=mesh, in_specs=in_specs, out_specs=out_specs, check_vma=False)
```
